128 devices in a mesh: leaf: 128 (over z, x, y, core).
Axes of the slice: x: 4, y: 4, z: 4, core: 2. Of those that a mesh axis runs over, the one named last changes fastest.
Arguments:
- coords: float32 [8192, 3, 128], P('leaf'), may hold values from -1 to 1
- areas: float32 [8192, 128], P('leaf'), may hold values from 0.01 to 0.1
- charges: float32 [8192, 32, 128], P('leaf'), may hold values from -6 to 6
- near_offsets: int32 [8192, 16], P('leaf'), may hold values from 0 to 16
- near_count: int32 [8192], P('leaf'), may hold values from 1 to 16
- far_offsets: int32 [8192, 8], P('leaf'), may hold values from 0 to 16
- far_coupling: float32 [8192, 8, 32, 32], P('leaf'), may hold values from -0.375 to 0.375
- basis: float32 [8192, 32, 128], P('leaf'), may hold values from -0.5 to 0.5
- root_transfer: float32 [8192, 32, 32], P('leaf'), may hold values from -0.125 to 0.125
- top_coupling: float32 [128, 128, 32, 32], P('leaf'), may hold values from -4 to 4
- task_source: int32 [16384, 1], replicated, may hold values from 0 to 127; in each aligned block of 128 rows (0 to 127, 128 to 255, ...) at most 2 rows name the same one
- task_row: int32 [16384], replicated, may hold values from 0 to 63
- task_col: int32 [16384], replicated, may hold values from 0 to 79
Outputs:
- potential: float32 [8192, 32, 128], P('leaf')
The draws below stay inside these ranges and needn't reach their ends.
Inputs may be any that keep to these rules, and one draw needn't show every extreme that they name: `task_source`: within each aligned block of 128 rows, no owner is named more than 2 times.
All inputs are finite; a program needn't handle non-finite values.
Results may differ from the reference program's by a relative error of at most 0.0003.
Values sent between devices are 32-bit elements; how exact they have to be, the bound alone decides.
No kernel may reach another device: no remote copies, remote signals or barrier semaphores. Data moves between devices by JAX's collectives and lax.ppermute only.
A program may use at most 128 MiB of HBM per device.

```python
import math
import jax
import jax.numpy as jnp
import numpy as np
from jax import lax

LEAF = 128
RANK = 32
RHS = 32
NEAR = 16
FAR = 8
HALO_LEAVES = 8
CAP = 2
LEAVES_DEV = 64
ROOTS = 128
TASK_DEV = 128
LEAVES = 8192
TASKS = 16384


def plant(result, rng, smallest, largest):
    longest = result.shape.index(max(result.shape))
    spots = []
    for shift in (0, 1):
        where = [jax.random.randint(jax.random.fold_in(rng, axis), (), 0, length) for axis, length in enumerate(result.shape)]
        where[longest] = (where[longest] + shift) % result.shape[longest]
        spots.append(tuple(where))
    return result.at[spots[0]].set(smallest).at[spots[1]].set(largest)


def with_spikes(drawn, stream_key, source, target, shards_of, factor):
    owner, partner = [(jnp.arange(drawn.shape[axis_at]) // (drawn.shape[axis_at] // shards_of)).reshape([-1 if axis == axis_at else 1 for axis in range(drawn.ndim)]) for axis_at in (source, target)]
    chosen = jax.random.permutation(stream_key, shards_of)[partner]
    strong = (owner == chosen) | (owner == (partner + shards_of // 2) % shards_of)
    return jnp.where(strong, factor * drawn, drawn)


def block_scale(rng, shape, pieces, low, largest):
    factor_of = 1.0
    for axis_at, parts in pieces:
        draws = jax.random.uniform(jax.random.fold_in(jax.random.fold_in(rng, 6), axis_at), (parts,), jnp.float32, low / len(pieces), largest / len(pieces))
        factor_of = factor_of * jnp.repeat(jnp.exp(draws), shape[axis_at] // parts).reshape((-1,) + (1,) * (len(shape) - 1 - axis_at))
    return factor_of


def shared_out(key, own, number, rows, count, top, most, lean):
    order = jax.random.permutation(key, count)
    heavy_load, ordinary = portions_of(count, rows * top, most, lean, True), portions_of(count, rows * top, most, lean, False)
    places = jnp.arange(count)

    def named(lengths, offset_by):
        used = int((lengths > 0).sum())
        fixed = max(1, used // 4)
        shifted = fixed + (places - fixed + offset_by * (used - fixed)) % max(1, count - fixed)
        return jnp.zeros((count,), jnp.int32).at[order[jnp.where(places < fixed, places, shifted)]].set(jnp.asarray(lengths, jnp.int32))

    lengths = jnp.where(number % 4 == 0, named(heavy_load, number // 4), named(ordinary, number - number // 4 - 1))
    mixed = jax.random.permutation(jax.random.fold_in(own, 3), count)
    giver, receiver = mixed[0:count // 2 * 2:2], mixed[1:count // 2 * 2:2]
    slack = jnp.minimum(lengths[giver] - 1, most - lengths[receiver]) // 2
    slack = jnp.where((giver == order[0]) | (receiver == order[0]) | (lengths[receiver] == 0), 0, jnp.maximum(slack, 0))
    shifted = jax.random.randint(jax.random.fold_in(own, 4), (count // 2,), 0, 1 << 20) % (slack + 1)
    lengths = lengths.at[giver].add(-shifted).at[receiver].add(shifted)
    items = jnp.searchsorted(jnp.cumsum(lengths), jnp.arange(rows * top), side="right").astype(jnp.int32)
    grid = items.reshape(top, rows).T
    grid = grid[jax.random.permutation(jax.random.fold_in(own, 1), rows)]
    offset_by = jax.random.randint(jax.random.fold_in(own, 2), (rows, 1), 0, top)
    return jnp.take_along_axis(grid, (jnp.arange(top)[None, :] + offset_by) % top, axis=1)


def portions_of(number_of, total, reach, slope, full):
    weights = [(1 << 20) // math.isqrt(grade ** slope) + 1 for grade in range(1, number_of + 1)]
    largest = reach if full else min(reach, max(-(-total // number_of), total * weights[0] // sum(weights)))
    least = 1 if total - largest >= number_of - 1 else 0
    given, surplus = [largest] + [least] * (number_of - 1), total - largest - least * (number_of - 1)
    while surplus > 0:
        free = [i for i in range(1, number_of) if given[i] < largest] or [i for i in range(1, number_of) if given[i] < reach]
        mass, remaining = sum([weights[i] for i in free]), surplus
        for i in free:
            more = min(reach - given[i], max(1, remaining * weights[i] // mass), surplus)
            given[i] = given[i] + more
            surplus = surplus - more
    return np.array(given)


def noise(rng, shape, spread, bound, split=(), kind=jnp.bfloat16):
    factor_of = block_scale(rng, shape, split, -0.22, 0.18) if split else 1.0
    result = jax.random.normal(rng, shape, jnp.float32) * spread * factor_of
    return jnp.minimum(jnp.maximum(result, -bound), bound).astype(kind)


def bell_draw_with(own_key, dims, spread, bound, shards, heavy, kind=jnp.bfloat16):
    array = spread * jax.random.normal(own_key, dims, jnp.float32)
    if shards:
        array = array * block_scale(own_key, dims, shards, -0.22, 0.18)
    return jnp.clip(with_spikes(array, jax.random.fold_in(own_key, 3), *heavy), -bound, bound).astype(kind)


def setup_inputs(seed: int = 0) -> dict:
    arg_keys = jax.random.split(jax.random.key(seed), 14)
    coords = jnp.clip(jax.random.uniform(arg_keys[0], (LEAVES, 3, LEAF), jnp.float32, -1.0, 1.0) * block_scale(arg_keys[0], (LEAVES, 3, LEAF), ((0, 128),), -0.4, 0.0), -1.0, 1.0)
    areas = jnp.clip(jnp.exp(math.log(0.1) - 2.3025851 * jax.random.uniform(arg_keys[1], (LEAVES, LEAF), jnp.float32) ** block_scale(arg_keys[1], (LEAVES, LEAF), ((0, 128),), -0.2, 0.2)), 0.01, 0.1)
    charges = noise(arg_keys[2], (LEAVES, RHS, LEAF), 1.0, 6.0, ((0, 128),), jnp.float32)
    near_offsets = plant(jax.random.randint(arg_keys[3], (LEAVES, NEAR), 0, 2 * HALO_LEAVES + 1), jax.random.fold_in(arg_keys[3], 1), 0, 2 * HALO_LEAVES).astype(jnp.int32)
    near_count = plant(jax.random.randint(arg_keys[4], (LEAVES,), 1, NEAR + 1), jax.random.fold_in(arg_keys[4], 1), 1, NEAR).astype(jnp.int32)
    far_offsets = plant(jax.random.randint(arg_keys[5], (LEAVES, FAR), 0, 2 * HALO_LEAVES + 1), jax.random.fold_in(arg_keys[5], 1), 0, 2 * HALO_LEAVES).astype(jnp.int32)
    far_coupling = noise(arg_keys[6], (LEAVES, FAR, RANK, RANK), (RANK * FAR) ** -0.5, 0.375, ((0, 128),), jnp.float32)
    basis = noise(arg_keys[7], (LEAVES, RANK, LEAF), LEAF ** -0.5, 0.5, ((0, 128),), jnp.float32)
    root_transfer = noise(arg_keys[8], (LEAVES, RANK, RANK), (RANK * LEAVES_DEV) ** -0.5, 0.125, ((0, 128),), jnp.float32)
    top_coupling = bell_draw_with(arg_keys[9], (ROOTS, ROOTS, RANK, RANK), RANK ** -0.5, 4.0, ((0, 128),), (1, 0, 128, 5.5), jnp.float32)
    task_source_keys = jax.random.split(jax.random.fold_in(arg_keys[10], 1), TASKS // TASK_DEV)
    task_source_turns = jax.random.permutation(jax.random.fold_in(arg_keys[10], 3), TASKS // TASK_DEV)
    task_source = jax.vmap(lambda own, number: shared_out(jax.random.fold_in(arg_keys[10], 2), own, number, TASK_DEV, ROOTS, 1, CAP, 2))(task_source_keys, task_source_turns).reshape((TASKS, 1))
    task_row = plant(jax.random.randint(arg_keys[11], (TASKS,), 0, LEAVES_DEV), jax.random.fold_in(arg_keys[11], 1), 0, LEAVES_DEV - 1).astype(jnp.int32)
    task_col = plant(jax.random.randint(arg_keys[12], (TASKS,), 0, LEAVES_DEV + 2 * HALO_LEAVES), jax.random.fold_in(arg_keys[12], 1), 0, (LEAVES_DEV + 2 * HALO_LEAVES) - 1).astype(jnp.int32)
    return {"coords": coords, "areas": areas, "charges": charges, "near_offsets": near_offsets, "near_count": near_count, "far_offsets": far_offsets, "far_coupling": far_coupling, "basis": basis, "root_transfer": root_transfer, "top_coupling": top_coupling, "task_source": task_source, "task_row": task_row, "task_col": task_col}


SOFTENING = 0.001
HIGHEST = lax.Precision.HIGHEST

def apply_kernel(row_points, column_points, column_area, column_charge):
    distance = jnp.zeros((row_points.shape[0], row_points.shape[2], column_points.shape[2]), jnp.float32)
    for component in range(3):
        offsets = row_points[:, component, :, None] - column_points[:, component, None, :]
        distance = distance + offsets * offsets
    kernel = column_area[:, None, :] / jnp.sqrt(distance + SOFTENING)
    return jnp.einsum('brj,bij->bri', column_charge, kernel, precision=HIGHEST)

def reference(coords, areas, charges, near_offsets, near_count, far_offsets, far_coupling, basis, root_transfer, top_coupling, task_source, task_row, task_col):
    leaf_ids = jnp.arange(LEAVES, dtype=jnp.int32)
    near_cols = jnp.clip(leaf_ids[:, None] - HALO_LEAVES + near_offsets, 0, LEAVES - 1).astype(jnp.int32)
    near_live = (jnp.arange(NEAR, dtype=jnp.int32)[None, :] < near_count[:, None]).astype(jnp.float32)

    def near_group(group):
        group_start = (group * LEAVES_DEV).astype(jnp.int32)
        row_points = lax.dynamic_slice_in_dim(coords, group_start, LEAVES_DEV, 0)
        column_ids = lax.dynamic_slice_in_dim(near_cols, group_start, LEAVES_DEV, 0).reshape(-1)
        weight = lax.dynamic_slice_in_dim(near_live, group_start, LEAVES_DEV, 0).reshape(-1)
        row_copies = jnp.repeat(row_points, NEAR, axis=0)
        blocks = apply_kernel(row_copies, coords[column_ids], areas[column_ids], charges[column_ids])
        blocks = blocks * weight[:, None, None]
        return lax.optimization_barrier(jnp.sum(blocks.reshape(LEAVES_DEV, NEAR, RHS, LEAF), axis=1))
    near_field = lax.map(near_group, jnp.arange(ROOTS, dtype=jnp.int32)).reshape(LEAVES, RHS, LEAF)
    owners = task_source[:, 0]
    task_rows = (owners * LEAVES_DEV + task_row).astype(jnp.int32)
    task_columns = jnp.clip(owners * LEAVES_DEV - HALO_LEAVES + task_col, 0, LEAVES - 1).astype(jnp.int32)

    def task_group(accumulated, group):
        group_start = (group * TASK_DEV).astype(jnp.int32)
        rows_here = lax.dynamic_slice_in_dim(task_rows, group_start, TASK_DEV, 0)
        columns_here = lax.dynamic_slice_in_dim(task_columns, group_start, TASK_DEV, 0)
        blocks = apply_kernel(coords[rows_here], coords[columns_here], areas[columns_here], charges[columns_here])
        return (accumulated.at[rows_here].add(blocks), None)
    near_field, trailing = lax.scan(task_group, near_field, jnp.arange(ROOTS, dtype=jnp.int32))
    coefficients = jnp.einsum('lrp,lkp->lrk', charges, basis, precision=HIGHEST)
    far_cols = jnp.clip(leaf_ids[:, None] - HALO_LEAVES + far_offsets, 0, LEAVES - 1).astype(jnp.int32)
    leaf_far = jnp.einsum('lfrk,lfkm->lrm', coefficients[far_cols], far_coupling, precision=HIGHEST)
    grouped_transfer = root_transfer.reshape(ROOTS, LEAVES_DEV, RANK, RANK)
    roots = jnp.einsum('dlrk,dlkm->drm', coefficients.reshape(ROOTS, LEAVES_DEV, RHS, RANK), grouped_transfer, precision=HIGHEST)
    root_field = jnp.einsum('erk,dekm->drm', roots, top_coupling, precision=HIGHEST)
    downward = jnp.einsum('drm,dlkm->dlrk', root_field, grouped_transfer, precision=HIGHEST).reshape(LEAVES, RHS, RANK)
    leaf_far = leaf_far + downward
    return near_field + jnp.einsum('lrk,lkp->lrp', leaf_far, basis, precision=HIGHEST)
```

```python
import functools

import jax
import jax.numpy as jnp
from jax import lax
from jax.experimental import pallas as pl
from jax.experimental.pallas import tpu as pltpu
from jax.sharding import PartitionSpec as P

HALO = 8
SOFTENING = 0.001
F32 = jnp.float32
BF16 = jnp.bfloat16
TERMS = 32
PACK = 72
NT = (((1,), (1,)), ((), ()))
NN = (((1,), (0,)), ((), ()))
TN = (((0,), (0,)), ((), ()))


def mm(a, b, dims=NN):
    return lax.dot_general(a, b, dims, preferred_element_type=F32)


def split(x):
    high = x.astype(BF16)
    return high, (x - high.astype(F32)).astype(BF16)


def stacked(x):
    high, low = split(x)
    top = jnp.concatenate([high, high], axis=1)
    bottom = jnp.concatenate([low, jnp.zeros_like(low)], axis=1)
    return jnp.concatenate([top, bottom], axis=0)


def lane_group(shape):
    return lax.broadcasted_iota(jnp.int32, shape, 1) // 32


def by_group(parts):
    group = lane_group(parts[0].shape)
    low = jnp.where(group == 0, parts[0], parts[1])
    high = jnp.where(group == 2, parts[2], parts[3])
    return jnp.where(group < 2, low, high)


def coefficients_rep(charge, base):
    high, low = split(base)
    both = jnp.concatenate([high, low], axis=1)
    both = jnp.concatenate([both] * 4, axis=0)
    out = mm(stacked(charge), both, NT)
    return out[:32] + out[32:]


def turned(x):
    return jnp.concatenate([x] * 4, axis=0).T[:32]


def group_sum(x):
    x = x + pltpu.roll(x, 64, 1)
    return x + pltpu.roll(x, 32, 1)


CHUNKS = 4
MANY = 32
FEW = 8


def roots_kernel(
    coords, areas, charges, basis, transfer, coeff, t_high, t_low, roots, head, tail, *scratch
):
    charge_v, basis_v, coeff_v, turned_v, t_high_v, t_low_v, roots_v, head_v, tail_v, in_sems, out_sems = scratch
    leaves = charges.shape[0]
    part = leaves // CHUNKS
    loads = []
    for c in range(CHUNKS):
        here = pl.ds(c * part, part)
        loads.append(
            (
                pltpu.make_async_copy(charges.at[here], charge_v.at[here], in_sems.at[2 * c]),
                pltpu.make_async_copy(basis.at[here], basis_v.at[here], in_sems.at[2 * c + 1]),
            )
        )
    for pair in loads:
        for copy in pair:
            copy.start()
    for h in range(8):
        rows = jnp.concatenate([transfer[8 * q + h] for q in range(4)], axis=0)
        turned_v[pl.ds(h, leaves, stride=8), :] = rows.T
    total = jnp.zeros((64, 128), F32)
    stores = []

    def four(g, total):
        parts = []
        for q in range(4):
            leaf = 4 * g + q
            value = coefficients_rep(charge_v[leaf], basis_v[leaf])
            coeff_v[leaf] = value
            parts.append(value)
            tile = turned_v[pl.ds(pl.multiple_of(8 * leaf, 8), 8), :]
            tile = jnp.concatenate([tile] + [pltpu.roll(tile, 128 - 32 * k, 1) for k in (1, 2, 3)], axis=0)
            high, low = split(tile)
            at = pl.ds(pl.multiple_of(32 * leaf, 32), 32)
            t_high_v[at, :] = high
            t_low_v[at, :] = low
        high, low = split(by_group(parts))
        at = pl.ds(pl.multiple_of(128 * g, 128), 128)
        total = total + mm(jnp.concatenate([high, low], axis=0), t_high_v[at, :])
        rest = mm(high, t_low_v[at, :])
        return total + jnp.concatenate([rest, jnp.zeros_like(rest)], axis=0)

    for c in range(CHUNKS):
        for copy in loads[c]:
            copy.wait()
        total = lax.fori_loop(c * part // 4, (c + 1) * part // 4, four, total, unroll=4)
        here = pl.ds(c * part, part)
        rows = pl.ds(c * part * 32, part * 32)
        for source, target in ((coeff_v.at[here], coeff.at[here]), (t_high_v.at[rows], t_high.at[rows]), (t_low_v.at[rows], t_low.at[rows])):
            copy = pltpu.make_async_copy(source, target, out_sems.at[len(stores)])
            copy.start()
            stores.append(copy)
        for at, out, out_v, first in ((0, head, head_v, 0), (CHUNKS - 1, tail, tail_v, leaves - HALO)):
            if c != at:
                continue
            for i in range(HALO):
                out_v[i, 0:32, :] = charge_v[first + i] * areas[pl.ds(first + i, 1), :]
                out_v[i, 32:64, :] = coeff_v[first + i]
            out_v[:, 64:72, :] = jnp.zeros((HALO, 8, 128), F32)
            for k in range(3):
                out_v[:, 64 + k, :] = coords[k, pl.ds(first, HALO), :]
            copy = pltpu.make_async_copy(out_v, out, out_sems.at[len(stores)])
            copy.start()
            stores.append(copy)
    total = turned(total[:32] + total[32:])
    packed = by_group([total[8 * g : 8 * g + 8] for g in range(4)])
    roots_v[...] = jnp.broadcast_to(packed[None], roots_v.shape)
    copy = pltpu.make_async_copy(roots_v, roots, out_sems.at[len(stores)])
    copy.start()
    for copy in stores + [copy]:
        copy.wait()


def terms(comps, rows):
    coarse = [jnp.floor(x * 128.0 + 0.5) * (1.0 / 128.0) for x in comps]
    fine = [x - q for x, q in zip(comps, coarse)]
    fine_high = [r.astype(BF16).astype(F32) for r in fine]
    fine_low = [r - h for r, h in zip(fine, fine_high)]
    square = sum(q * q for q in coarse)
    square_high = square.astype(BF16).astype(F32)
    square_low = square - square_high
    rest = sum(2.0 * q * r + r * r for q, r in zip(coarse, fine))
    if rows:
        rest = rest + SOFTENING
    rest_1 = rest.astype(BF16).astype(F32)
    rest_2 = (rest - rest_1).astype(BF16).astype(F32)
    rest_3 = rest - rest_1 - rest_2
    one = jnp.ones_like(square)
    zero = jnp.zeros_like(square)
    if rows:
        coarse = [-2.0 * x for x in coarse]
        fine_high = [-2.0 * x for x in fine_high]
        fine_low = [-2.0 * x for x in fine_low]
        own = [square_high, square_low, one, one]
        own2 = [rest_1, rest_2, rest_3, one, one, one]
        return own + coarse + [zero] + own2 + fine_high + fine_low + coarse + coarse + fine_high + fine_low
    own = [one, one, square_high, square_low]
    own2 = [one, one, one, rest_1, rest_2, rest_3]
    return own + coarse + [zero] + own2 + coarse + coarse + fine_high + fine_low + fine_high + fine_high


def high_low(x):
    high = x.astype(BF16).astype(F32)
    return jnp.where(lane_group(x.shape) < 2, high, x - high)


def build_lists(position, leaves, leaf_total, near_offsets, near_count, task_source, task_row, task_col, codes):
    first = position * leaves
    low, high = HALO - first, leaf_total - 1 - first + HALO
    slots = near_offsets.shape[0]
    shape = (128, 128)
    column = lax.broadcasted_iota(jnp.int32, shape, 0)
    row = lax.broadcasted_iota(jnp.int32, shape, 1)
    spare = 128 - leaves
    offsets = jnp.concatenate([near_offsets[...], jnp.zeros((slots, spare), jnp.int32)], axis=1)
    count = jnp.concatenate([near_count[...], jnp.zeros((1, spare), jnp.int32)], axis=1)
    near = jnp.zeros(shape, F32)
    for s in range(slots):
        at = jnp.clip(offsets[s : s + 1] + row[0:1], low, high)
        at = jnp.where(count > s, at, -1)
        near = near + jnp.where(column == at, 1.0, 0.0)
    mine = task_source[...] == position
    at = jnp.clip(task_col[...], low, high)
    value = jnp.where(mine, task_row[...] * 128 + at + 1, 0).astype(F32)
    largest = jnp.max(value, axis=1, keepdims=True)
    other = jnp.sum(value, axis=1, keepdims=True) - largest
    listed = jnp.zeros(shape, F32)
    lanes = lax.broadcasted_iota(jnp.int32, (value.shape[0], 128), 1)
    for value in (largest, other):
        task = value.astype(jnp.int32) - 1
        t_row = jnp.where(task < 0, -1, task // 128)
        t_col = jnp.where(task < 0, -1, task % 128)
        pick_row = jnp.where(lanes == t_row, 1.0, 0.0).astype(BF16)
        pick_col = jnp.where(lanes == t_col, 1.0, 0.0).astype(BF16)
        listed = listed + mm(pick_col, pick_row, TN)
    used = jnp.where(near + listed > 0.0, 1.0, 0.0)
    before = jnp.where(column < row, 1.0, 0.0).astype(BF16)
    rank = mm(used.astype(BF16), before)
    number = jnp.sum(used, axis=1, keepdims=True)
    pairs = jnp.floor((number + 1.0) * 0.5)
    after = jnp.where(row <= column, 1.0, 0.0).astype(BF16)
    pairs_wide = jnp.broadcast_to(pairs, shape)
    ends = mm(after, pairs_wide.astype(BF16))
    size = codes.shape[1]
    copies = size // 128
    ends_wide = jnp.concatenate([ends] * copies, axis=1)
    starts_wide = jnp.concatenate([ends - pairs_wide] * copies, axis=1)
    place = lax.broadcasted_iota(jnp.int32, (128, size), 1).astype(F32)
    here = jnp.where((place >= starts_wide) & (place < ends_wide), 1.0, 0.0)
    column_at = jnp.sum(jnp.where(place >= ends_wide, 1.0, 0.0), axis=0, keepdims=True)
    within = jnp.sum(here * (place - starts_wide), axis=0, keepdims=True)
    here = here.astype(BF16)
    order = (used * (rank + 1.0)).T.astype(BF16)[:leaves]
    near_t = near.T.astype(BF16)[:leaves]
    listed_t = listed.T.astype(BF16)[:leaves]
    order_at = mm(order, here)
    weight_at = mm(near_t, here) + mm(listed_t, here)
    row_at = lax.broadcasted_iota(jnp.int32, (leaves, size), 0).astype(F32)
    found = []
    for k in (1.0, 2.0):
        hit = order_at == (2.0 * within + k)
        found.append(leaves + jnp.sum(jnp.where(hit, row_at - leaves, 0.0), axis=0, keepdims=True))
        found.append(jnp.sum(jnp.where(hit, weight_at, 0.0), axis=0, keepdims=True))
    row_1, weight_1, row_2, weight_2 = [x.astype(jnp.int32) for x in found]
    total = jnp.concatenate([ends[127:128]] * copies, axis=1).astype(jnp.int32)
    column_at = jnp.minimum(column_at.astype(jnp.int32), leaves + 2 * HALO - 1)
    codes[0:1, :] = column_at * 65536 + row_1 * 256 + row_2
    codes[1:2, :] = weight_1 * 65536 + weight_2
    codes[2:3, :] = total
    codes[3:8, :] = jnp.zeros((5, size), jnp.int32)


def near_kernel(
    leaf_total,
    place,
    far_offsets,
    coords,
    areas,
    charges,
    coeff,
    left_h,
    right_h,
    near_offsets,
    near_count,
    task_source,
    task_row,
    task_col,
    coupling,
    field,
    far,
    rows_f,
    cols_f,
    rows_b,
    cols_b,
    weighted,
    ext,
    coupling_v,
    turned_v,
    left,
    right,
    codes,
    codes_s,
    sems,
):
    leaves = charges.shape[0]
    wide = leaves + 2 * HALO
    position = place[0]
    left_copy = pltpu.make_async_copy(left_h, left, sems.at[2])
    right_copy = pltpu.make_async_copy(right_h, right, sems.at[3])
    left_copy.start()
    right_copy.start()
    coupling_copy = pltpu.make_async_copy(coupling, coupling_v, sems.at[0])
    coupling_copy.start()
    build_lists(
        position, leaves, leaf_total, near_offsets, near_count, task_source, task_row, task_col, codes
    )
    codes_copy = pltpu.make_async_copy(codes, codes_s, sems.at[1])
    codes_copy.start()
    field[...] = jnp.zeros_like(field)

    mine = [coords[c] for c in range(3)]
    for k, value in enumerate(terms(mine, True)):
        rows_f[pl.ds(k, leaves, stride=TERMS), :] = value
    rows_b[pl.ds(0, leaves * TERMS), :] = rows_f[...].astype(BF16)
    rows_b[pl.ds(leaves * TERMS, TERMS), :] = rows_f[0:TERMS, :].astype(BF16)
    left_copy.wait()
    right_copy.wait()
    everyone = [
        jnp.concatenate([left[:, 64 + c, :], mine[c], right[:, 64 + c, :]], axis=0) for c in range(3)
    ]
    for k, value in enumerate(terms(everyone, False)):
        cols_f[pl.ds(k, wide, stride=TERMS), :] = value
    eye = jnp.where(
        lax.broadcasted_iota(jnp.int32, (128, 128), 0) == lax.broadcasted_iota(jnp.int32, (128, 128), 1),
        1.0,
        0.0,
    ).astype(BF16)

    def turn(g, carry):
        block = cols_f[pl.ds(pl.multiple_of(g * 128, 128), 128), :].astype(BF16)
        out = mm(eye, block, NT)
        for q in range(4):
            cols_b[4 * g + q] = out[:, 32 * q : 32 * q + 32].astype(BF16)
        return carry

    lax.fori_loop(0, wide // 4, turn, 0, unroll=10)

    for i in range(HALO):
        weighted[i] = stacked(left[i, 0:32, :])
        weighted[wide - HALO + i] = stacked(right[i, 0:32, :])
        ext[i] = high_low(left[i, 32:64, :])
        ext[wide - HALO + i] = high_low(right[i, 32:64, :])

    def weigh(i, carry):
        weighted[HALO + i] = stacked(charges[i] * areas[pl.ds(i, 1), :])
        ext[HALO + i] = high_low(coeff[i])
        return carry

    lax.fori_loop(0, leaves, weigh, 0, unroll=8)
    codes_copy.wait()
    number = codes_s[2, 0]

    def pair(p):
        code = codes_s[0, p]
        weights = codes_s[1, p]
        column = code // 65536
        row_1 = (code // 256) % 256
        row_2 = code % 256
        points = cols_b[column]
        x_1 = rows_b[pl.ds(pl.multiple_of(row_1 * TERMS, TERMS), TERMS), :]
        x_2 = rows_b[pl.ds(pl.multiple_of(row_2 * TERMS, TERMS), TERMS), :]
        square = mm(points, jnp.concatenate([x_1, x_2], axis=1))
        inverse = lax.rsqrt(square)
        high, low = split(inverse)
        out = mm(weighted[column], jnp.concatenate([high, low], axis=0))
        out = out[:32] + out[32:]
        w_1 = (weights // 65536).astype(F32)
        w_2 = (weights % 65536).astype(F32)
        return row_1, out[:, :128] * w_1, row_2, out[:, 128:] * w_2

    def several(first, width, step, carry):
        done = [pair(first + step * width + u) for u in range(width)]
        for row_1, out_1, row_2, out_2 in done:
            field[row_1] += out_1
            field[row_2] += out_2
        return carry

    many = number // MANY
    lax.fori_loop(0, many, functools.partial(several, 0, MANY), 0)
    others = (number - many * MANY + FEW - 1) // FEW
    lax.fori_loop(0, others, functools.partial(several, many * MANY, FEW), 0)

    coupling_copy.wait()
    first = position * leaves
    low_at, high_at = HALO - first, leaf_total - 1 - first + HALO

    def turn_coupling(k, carry):
        for h in range(2):
            rows = jnp.concatenate([coupling_v[4 * h + q, k] for q in range(4)], axis=0)
            turned_v[pl.ds(32 * h + k, leaves, stride=64), :] = rows.T
        return carry

    lax.fori_loop(0, 32, turn_coupling, 0, unroll=8)

    def far_leaf(leaf):
        parts = [ext[jnp.clip(leaf + far_offsets[f, leaf], low_at, high_at)] for f in range(8)]
        even = lane_group(parts[0].shape) % 2 == 0
        rows = [jnp.where(even, parts[f], parts[4 + f]) for f in range(4)]
        rows = jnp.concatenate(rows, axis=0).astype(BF16)
        high, low = split(turned_v[pl.ds(pl.multiple_of(64 * leaf, 64), 64), :])
        out = mm(
            jnp.concatenate([rows, rows], axis=1),
            jnp.concatenate([high, high, low, low], axis=0),
        )
        return group_sum(by_group([out[32 * q : 32 * q + 32] for q in range(4)]))

    def far_four(g, carry):
        far[g] = by_group([far_leaf(4 * g + q) for q in range(4)])
        return carry

    lax.fori_loop(0, leaves // 4, far_four, 0, unroll=8)


def final_kernel(portion, top, t_high, t_low, basis, near, far, out, *scratch):
    portion_v, top_v, t_high_v, t_low_v, basis_v, near_v, far_v, out_v, sems, out_sems = scratch
    leaves = basis.shape[0]
    copies = [
        pltpu.make_async_copy(source, target, sems.at[i])
        for i, (source, target) in enumerate(
            (
                (portion, portion_v),
                (top, top_v),
                (t_high, t_high_v),
                (t_low, t_low_v),
                (far, far_v),
                (basis, basis_v),
                (near.at[pl.ds(0, leaves)], near_v),
            )
        )
    ]
    for copy in copies:
        copy.start()
    copies[0].wait()
    copies[1].wait()
    total = jnp.zeros((128, 128), F32)
    for s in range(0, 8, 2):
        blocks = [jnp.concatenate([top_v[8 * q + s + i] for q in range(4)], axis=0) for i in range(2)]
        c_high, c_low = split(jnp.concatenate(blocks, axis=1))
        p_high, p_low = split(jnp.concatenate([portion_v[:, s + i, :] for i in range(2)], axis=0))
        both = mm(jnp.concatenate([c_high, c_low], axis=0), p_high)
        total = total + both[:128] + both[128:] + mm(c_high, p_low)
    root = turned(group_sum(by_group([total[32 * q : 32 * q + 32] for q in range(4)])))
    root = jnp.where(lane_group(root.shape) == 0, root, 0.0)
    root_high, root_low = split(root)
    roots = jnp.concatenate([root_high, root_low], axis=0)
    for copy in copies[2:]:
        copy.wait()

    def final(g, carry):
        at = pl.ds(pl.multiple_of(128 * g, 128), 128)
        down = mm(roots, t_high_v[at, :], NT)
        down = down[:32] + down[32:] + mm(root_high, t_low_v[at, :], NT)
        value = far_v[g] + down
        group = lane_group(value.shape)
        spread = jnp.concatenate([jnp.where(group == q, value, 0.0) for q in range(4)], axis=0)
        high, low = split(spread)
        b_high, b_low = split(basis_v[pl.ds(4 * g, 4)].reshape(128, 128))
        res = mm(jnp.concatenate([high, low], axis=1), jnp.concatenate([b_high, b_high], axis=0))
        res = res + mm(high, b_low)
        out_v[pl.ds(4 * g, 4)] = near_v[pl.ds(4 * g, 4)] + res.reshape(4, 32, 128)
        return carry

    stores = []
    part = leaves // CHUNKS
    for c in range(CHUNKS):
        lax.fori_loop(c * part // 4, (c + 1) * part // 4, final, 0, unroll=4)
        here = pl.ds(c * part, part)
        stores.append(pltpu.make_async_copy(out_v.at[here], out.at[here], out_sems.at[c]))
        stores[-1].start()
    for copy in stores:
        copy.wait()


VMEM = pl.BlockSpec(memory_space=pltpu.VMEM)
SMEM = pl.BlockSpec(memory_space=pltpu.SMEM)
ANY = pl.BlockSpec(memory_space=pltpu.HBM)
PARAMS = pltpu.CompilerParams(vmem_limit_bytes=56 * 1024 * 1024)


def struct(*shape, dtype=F32):
    return jax.ShapeDtypeStruct(shape, dtype)


def local(
    coords,
    areas,
    charges,
    near_offsets,
    near_count,
    far_offsets,
    far_coupling,
    basis,
    root_transfer,
    top_coupling,
    task_source,
    task_row,
    task_col,
):
    devices = lax.axis_size("leaf")
    position = lax.axis_index("leaf")
    leaves = coords.shape[0]
    wide = leaves + 2 * HALO
    coords = coords.transpose(1, 0, 2)
    transfer = root_transfer.transpose(1, 2, 0)
    top = top_coupling[0].transpose(1, 2, 0)
    coupling = far_coupling.transpose(1, 2, 3, 0)
    rows = leaves * 32
    coeff, t_high, t_low, roots, head, tail = pl.pallas_call(
        roots_kernel,
        out_shape=[
            struct(leaves, 32, 128),
            struct(rows, 128, dtype=BF16),
            struct(rows, 128, dtype=BF16),
            struct(devices, 8, 128),
            struct(HALO, PACK, 128),
            struct(HALO, PACK, 128),
        ],
        in_specs=[VMEM, VMEM, ANY, ANY, VMEM],
        out_specs=[ANY] * 6,
        scratch_shapes=[
            pltpu.VMEM((leaves, 32, 128), F32),
            pltpu.VMEM((leaves, 32, 128), F32),
            pltpu.VMEM((leaves, 32, 128), F32),
            pltpu.VMEM((leaves * 8, 128), F32),
            pltpu.VMEM((rows, 128), BF16),
            pltpu.VMEM((rows, 128), BF16),
            pltpu.VMEM((devices, 8, 128), F32),
            pltpu.VMEM((HALO, PACK, 128), F32),
            pltpu.VMEM((HALO, PACK, 128), F32),
            pltpu.SemaphoreType.DMA((2 * CHUNKS,)),
            pltpu.SemaphoreType.DMA((3 * CHUNKS + 3,)),
        ],
        compiler_params=PARAMS,
        name="coefficients",
    )(coords, areas, charges, basis, transfer)
    left = lax.ppermute(tail, "leaf", [(i, (i + 1) % devices) for i in range(devices)])
    right = lax.ppermute(head, "leaf", [((i + 1) % devices, i) for i in range(devices)])
    portion = lax.all_to_all(roots, "leaf", 0, 0, tiled=True)
    near, far = pl.pallas_call(
        functools.partial(near_kernel, leaves * devices),
        out_shape=[struct(leaves + 8, 32, 128), struct(leaves // 4, 32, 128)],
        in_specs=[SMEM, SMEM] + [VMEM] * 4 + [ANY, ANY] + [VMEM] * 5 + [ANY],
        out_specs=[VMEM] * 2,
        scratch_shapes=[
            pltpu.VMEM((leaves * TERMS, 128), F32),
            pltpu.VMEM((wide * TERMS, 128), F32),
            pltpu.VMEM(((leaves + 1) * TERMS, 128), BF16),
            pltpu.VMEM((wide, 128, 32), BF16),
            pltpu.VMEM((wide, 64, 256), BF16),
            pltpu.VMEM((wide, 32, 128), F32),
            pltpu.VMEM((8, 32, 32, leaves), F32),
            pltpu.VMEM((leaves * 64, 128), F32),
            pltpu.VMEM((HALO, PACK, 128), F32),
            pltpu.VMEM((HALO, PACK, 128), F32),
            pltpu.VMEM((8, 768), jnp.int32),
            pltpu.SMEM((8, 768), jnp.int32),
            pltpu.SemaphoreType.DMA((4,)),
        ],
        compiler_params=PARAMS,
        cost_estimate=pl.CostEstimate(flops=3 * 10**10, bytes_accessed=3 * 10**7, transcendentals=10**7),
        name="near",
    )(
        position.reshape(1),
        far_offsets.T,
        coords,
        areas,
        charges,
        coeff,
        left,
        right,
        near_offsets.T,
        near_count.reshape(1, leaves),
        task_source.reshape(devices, -1),
        task_row.reshape(devices, -1),
        task_col.reshape(devices, -1),
        coupling,
    )
    return pl.pallas_call(
        final_kernel,
        out_shape=struct(leaves, 32, 128),
        in_specs=[ANY] * 7,
        out_specs=ANY,
        scratch_shapes=[
            pltpu.VMEM((devices, 8, 128), F32),
            pltpu.VMEM((32, 32, devices), F32),
            pltpu.VMEM((rows, 128), BF16),
            pltpu.VMEM((rows, 128), BF16),
            pltpu.VMEM((leaves, 32, 128), F32),
            pltpu.VMEM((leaves, 32, 128), F32),
            pltpu.VMEM((leaves // 4, 32, 128), F32),
            pltpu.VMEM((leaves, 32, 128), F32),
            pltpu.SemaphoreType.DMA((7,)),
            pltpu.SemaphoreType.DMA((CHUNKS,)),
        ],
        compiler_params=PARAMS,
        name="final",
    )(portion, top, t_high, t_low, basis, near, far)


def solution(mesh):
    placed = (
        P("leaf", None, None),
        P("leaf", None),
        P("leaf", None, None),
        P("leaf", None),
        P("leaf"),
        P("leaf", None),
        P("leaf", None, None, None),
        P("leaf", None, None),
        P("leaf", None, None),
        P("leaf", None, None, None),
        P(),
        P(),
        P(),
    )
    return jax.shard_map(
        local, mesh=mesh, in_specs=placed, out_specs=P("leaf", None, None), check_vma=False
    )
```

```python
import functools

import jax
import jax.numpy as jnp
from jax import lax
from jax.experimental import pallas as pl
from jax.experimental.pallas import tpu as pltpu
from jax.sharding import PartitionSpec as P

HALO = 8
SOFTENING = 0.001
F32 = jnp.float32
BF16 = jnp.bfloat16
TERMS = 32
PACK = 48
NT = (((1,), (1,)), ((), ()))
NN = (((1,), (0,)), ((), ()))
TN = (((0,), (0,)), ((), ()))


def mm(a, b, dims=NN):
    return lax.dot_general(a, b, dims, preferred_element_type=F32)


def split(x):
    high = x.astype(BF16)
    return high, (x - high.astype(F32)).astype(BF16)


def stacked(x):
    high, low = split(x)
    top = jnp.concatenate([high, high], axis=1)
    bottom = jnp.concatenate([low, jnp.zeros_like(low)], axis=1)
    return jnp.concatenate([top, bottom], axis=0)


def lane_group(shape):
    return lax.broadcasted_iota(jnp.int32, shape, 1) // 32


def by_group(parts):
    group = lane_group(parts[0].shape)
    low = jnp.where(group == 0, parts[0], parts[1])
    high = jnp.where(group == 2, parts[2], parts[3])
    return jnp.where(group < 2, low, high)


def turned(x):
    return jnp.concatenate([x] * 4, axis=0).T[:32]


def group_sum(x):
    x = x + pltpu.roll(x, 64, 1)
    return x + pltpu.roll(x, 32, 1)


CHUNKS = 2
WIDTHS = (64, 16, 4)
FAR_ROOM = 3200


def roots_kernel(
    coords, areas, charges, basis, transfer, coeff, t_high, t_low, roots, head, tail, *scratch
):
    charge_v, basis_v, coeff_v, turned_v, t_high_v, t_low_v, roots_v, head_v, tail_v, in_sems, out_sems = scratch
    leaves = charges.shape[0]
    part = leaves // CHUNKS
    loads = []
    for c in range(CHUNKS):
        here = pl.ds(c * part, part)
        loads.append(
            (
                pltpu.make_async_copy(charges.at[here], charge_v.at[here], in_sems.at[2 * c]),
                pltpu.make_async_copy(basis.at[here], basis_v.at[here], in_sems.at[2 * c + 1]),
            )
        )
    for pair in loads:
        for copy in pair:
            copy.start()
    for h in range(8):
        rows = jnp.concatenate([transfer[8 * q + h] for q in range(4)], axis=0)
        turned_v[pl.ds(h, leaves, stride=8), :] = rows.T
    total = jnp.zeros((64, 128), F32)
    stores = []

    def four(g, total):
        leaf = 4 * g
        values = jnp.concatenate([stacked(charge_v[leaf + q]) for q in range(4)], axis=0)
        bases = jnp.concatenate(split(basis_v[pl.ds(leaf, 4)].reshape(128, 128)), axis=1)
        out = mm(values, bases, NT)
        value = by_group([out[64 * q : 64 * q + 32] + out[64 * q + 32 : 64 * q + 64] for q in range(4)])
        coeff_v[g] = value
        for q in range(4):
            tile = turned_v[pl.ds(pl.multiple_of(8 * (leaf + q), 8), 8), :]
            tile = jnp.concatenate([tile] + [pltpu.roll(tile, 128 - 32 * k, 1) for k in (1, 2, 3)], axis=0)
            high, low = split(tile)
            at = pl.ds(pl.multiple_of(32 * (leaf + q), 32), 32)
            t_high_v[at, :] = high
            t_low_v[at, :] = low
        high, low = split(value)
        at = pl.ds(pl.multiple_of(128 * g, 128), 128)
        total = total + mm(jnp.concatenate([high, low], axis=0), t_high_v[at, :])
        rest = mm(high, t_low_v[at, :])
        return total + jnp.concatenate([rest, jnp.zeros_like(rest)], axis=0)

    for c in range(CHUNKS):
        for copy in loads[c]:
            copy.wait()
        total = lax.fori_loop(c * part // 4, (c + 1) * part // 4, four, total, unroll=8)
        here = pl.ds(c * part // 4, part // 4)
        rows = pl.ds(c * part * 32, part * 32)
        for source, target in ((coeff_v.at[here], coeff.at[here]), (t_high_v.at[rows], t_high.at[rows]), (t_low_v.at[rows], t_low.at[rows])):
            copy = pltpu.make_async_copy(source, target, out_sems.at[len(stores)])
            copy.start()
            stores.append(copy)
    for out, out_v, first in ((head, head_v, 0), (tail, tail_v, leaves - HALO)):
        for i in range(HALO):
            out_v[i, 0:32, :] = charge_v[first + i] * areas[pl.ds(first + i, 1), :]
            out_v[i, 40:48, :] = coeff_v[first // 4 + i // 4, pl.ds(8 * (i % 4), 8), :]
        out_v[:, 32:40, :] = jnp.zeros((HALO, 8, 128), F32)
        for k in range(3):
            out_v[:, 32 + k, :] = coords[k, pl.ds(first, HALO), :]
        copy = pltpu.make_async_copy(out_v, out, out_sems.at[len(stores)])
        copy.start()
        stores.append(copy)
    total = turned(total[:32] + total[32:])
    packed = by_group([total[8 * g : 8 * g + 8] for g in range(4)])
    roots_v[...] = jnp.broadcast_to(packed[None], roots_v.shape)
    copy = pltpu.make_async_copy(roots_v, roots, out_sems.at[len(stores)])
    copy.start()
    for copy in stores + [copy]:
        copy.wait()


def terms(comps, rows):
    coarse = [jnp.floor(x * 128.0 + 0.5) * (1.0 / 128.0) for x in comps]
    fine = [x - q for x, q in zip(comps, coarse)]
    fine_high = [r.astype(BF16).astype(F32) for r in fine]
    fine_low = [r - h for r, h in zip(fine, fine_high)]
    square = sum(q * q for q in coarse)
    square_high = square.astype(BF16).astype(F32)
    square_low = square - square_high
    rest = sum(2.0 * q * r + r * r for q, r in zip(coarse, fine))
    if rows:
        rest = rest + SOFTENING
    rest_1 = rest.astype(BF16).astype(F32)
    rest_2 = (rest - rest_1).astype(BF16).astype(F32)
    rest_3 = rest - rest_1 - rest_2
    one = jnp.ones_like(square)
    zero = jnp.zeros_like(square)
    if rows:
        coarse = [-2.0 * x for x in coarse]
        fine_high = [-2.0 * x for x in fine_high]
        fine_low = [-2.0 * x for x in fine_low]
        own = [square_high, square_low, one, one]
        own2 = [rest_1, rest_2, rest_3, one, one, one]
        return own + coarse + [zero] + own2 + fine_high + fine_low + coarse + coarse + fine_high + fine_low
    own = [one, one, square_high, square_low]
    own2 = [one, one, one, rest_1, rest_2, rest_3]
    return own + coarse + [zero] + own2 + coarse + coarse + fine_high + fine_low + fine_high + fine_high


def build_lists(position, leaves, leaf_total, near_offsets, near_count, task_source, task_row, task_col, codes):
    first = position * leaves
    low, high = HALO - first, leaf_total - 1 - first + HALO
    slots = near_offsets.shape[0]
    shape = (128, 128)
    column = lax.broadcasted_iota(jnp.int32, shape, 0)
    row = lax.broadcasted_iota(jnp.int32, shape, 1)
    spare = 128 - leaves
    offsets = jnp.concatenate([near_offsets[...], jnp.zeros((slots, spare), jnp.int32)], axis=1)
    count = jnp.concatenate([near_count[...], jnp.zeros((1, spare), jnp.int32)], axis=1)
    near = jnp.zeros(shape, F32)
    for s in range(slots):
        at = jnp.clip(offsets[s : s + 1] + row[0:1], low, high)
        at = jnp.where(count > s, at, -1)
        near = near + jnp.where(column == at, 1.0, 0.0)
    mine = task_source[...] == position
    at = jnp.clip(task_col[...], low, high)
    value = jnp.where(mine, task_row[...] * 128 + at + 1, 0).astype(F32)
    largest = jnp.max(value, axis=1, keepdims=True)
    other = jnp.sum(value, axis=1, keepdims=True) - largest
    listed = jnp.zeros(shape, F32)
    lanes = lax.broadcasted_iota(jnp.int32, (value.shape[0], 128), 1)
    for value in (largest, other):
        task = value.astype(jnp.int32) - 1
        t_row = jnp.where(task < 0, -1, task // 128)
        t_col = jnp.where(task < 0, -1, task % 128)
        pick_row = jnp.where(lanes == t_row, 1.0, 0.0).astype(BF16)
        pick_col = jnp.where(lanes == t_col, 1.0, 0.0).astype(BF16)
        listed = listed + mm(pick_col, pick_row, TN)
    used = jnp.where(near + listed > 0.0, 1.0, 0.0)
    before = jnp.where(column < row, 1.0, 0.0).astype(BF16)
    rank = mm(used.astype(BF16), before)
    number = jnp.sum(used, axis=1, keepdims=True)
    pairs = jnp.floor((number + 1.0) * 0.5)
    after = jnp.where(row <= column, 1.0, 0.0).astype(BF16)
    pairs_wide = jnp.broadcast_to(pairs, shape)
    ends = mm(after, pairs_wide.astype(BF16))
    size = codes.shape[1]
    copies = size // 128
    ends_wide = jnp.concatenate([ends] * copies, axis=1)
    starts_wide = jnp.concatenate([ends - pairs_wide] * copies, axis=1)
    place = lax.broadcasted_iota(jnp.int32, (128, size), 1).astype(F32)
    here = jnp.where((place >= starts_wide) & (place < ends_wide), 1.0, 0.0)
    column_at = jnp.sum(jnp.where(place >= ends_wide, 1.0, 0.0), axis=0, keepdims=True)
    within = jnp.sum(here * (place - starts_wide), axis=0, keepdims=True)
    here = here.astype(BF16)
    order = (used * (rank + 1.0)).T.astype(BF16)[:leaves]
    near_t = near.T.astype(BF16)[:leaves]
    listed_t = listed.T.astype(BF16)[:leaves]
    order_at = mm(order, here)
    weight_at = mm(near_t, here) + mm(listed_t, here)
    row_at = lax.broadcasted_iota(jnp.int32, (leaves, size), 0).astype(F32)
    found = []
    for k in (1.0, 2.0):
        hit = order_at == (2.0 * within + k)
        found.append(leaves + jnp.sum(jnp.where(hit, row_at - leaves, 0.0), axis=0, keepdims=True))
        found.append(jnp.sum(jnp.where(hit, weight_at, 0.0), axis=0, keepdims=True))
    row_1, weight_1, row_2, weight_2 = [x.astype(jnp.int32) for x in found]
    total = jnp.concatenate([ends[127:128]] * copies, axis=1).astype(jnp.int32)
    column_at = jnp.minimum(column_at.astype(jnp.int32), leaves + 2 * HALO - 1)
    codes[0:1, :] = column_at * 65536 + row_1 * 256 + row_2
    codes[1:2, :] = weight_1 * 65536 + weight_2
    codes[2:3, :] = total
    codes[3:8, :] = jnp.zeros((5, size), jnp.int32)


def near_kernel(
    leaf_total,
    place,
    far_offsets,
    coords,
    areas,
    charges_h,
    coeff_h,
    left_h,
    right_h,
    near_offsets,
    near_count,
    task_source,
    task_row,
    task_col,
    coupling,
    field_h,
    far_h,
    far,
    field,
    charges,
    coeff,
    rows_f,
    cols_f,
    rows_b,
    cols_b,
    weighted,
    ext,
    coupling_v,
    turned_v,
    halo,
    codes,
    codes_s,
    sems,
):
    leaves = charges.shape[0]
    wide = leaves + 2 * HALO
    position = place[0]
    charges_copy = pltpu.make_async_copy(charges_h, charges, sems.at[4])
    coeff_copy = pltpu.make_async_copy(coeff_h, coeff, sems.at[5])
    charges_copy.start()
    coeff_copy.start()
    left, right = halo.at[0], halo.at[1]
    left_copy = pltpu.make_async_copy(left_h, left, sems.at[2])
    right_copy = pltpu.make_async_copy(right_h, right, sems.at[3])
    left_copy.start()
    right_copy.start()
    coupling_copy = pltpu.make_async_copy(coupling, coupling_v, sems.at[0])
    coupling_copy.start()
    build_lists(
        position, leaves, leaf_total, near_offsets, near_count, task_source, task_row, task_col, codes
    )
    codes_copy = pltpu.make_async_copy(codes, codes_s, sems.at[1])
    codes_copy.start()
    field[...] = jnp.zeros_like(field)

    mine = [coords[c] for c in range(3)]
    for k, value in enumerate(terms(mine, True)):
        rows_f[pl.ds(k, leaves, stride=TERMS), :] = value
    rows_b[pl.ds(0, leaves * TERMS), :] = rows_f[...].astype(BF16)
    rows_b[pl.ds(leaves * TERMS, TERMS), :] = rows_f[0:TERMS, :].astype(BF16)
    left_copy.wait()
    right_copy.wait()
    everyone = [
        jnp.concatenate([left[:, 32 + c, :], mine[c], right[:, 32 + c, :]], axis=0) for c in range(3)
    ]
    for k, value in enumerate(terms(everyone, False)):
        cols_f[pl.ds(k, wide, stride=TERMS), :] = value
    eye = jnp.where(
        lax.broadcasted_iota(jnp.int32, (128, 128), 0) == lax.broadcasted_iota(jnp.int32, (128, 128), 1),
        1.0,
        0.0,
    ).astype(BF16)

    def turn(g, carry):
        block = cols_f[pl.ds(pl.multiple_of(g * 128, 128), 128), :].astype(BF16)
        out = mm(eye, block, NT)
        for q in range(4):
            cols_b[4 * g + q] = jnp.where(lane_group(out.shape) == q, out, 0.0).astype(BF16)
        return carry

    lax.fori_loop(0, wide // 4, turn, 0, unroll=10)

    source = lax.broadcasted_iota(jnp.int32, (256, 512), 0)
    target = lax.broadcasted_iota(jnp.int32, (256, 512), 1)
    same = (source % 32 == target % 32) & ((source % 128) // 32 == target // 128)
    same = same & (source // 128 == (target % 128) // 64)
    spread = jnp.where(same, 1.0, 0.0).astype(BF16)

    def expand(first, packed):
        out = mm(jnp.concatenate(split(packed), axis=1), spread)
        for q in range(4):
            ext[first + q] = out[:, 128 * q : 128 * q + 128]

    for i in range(HALO):
        weighted[i] = stacked(left[i, 0:32, :])
        weighted[wide - HALO + i] = stacked(right[i, 0:32, :])
    for i in range(0, HALO, 4):
        expand(i, left[pl.ds(i, 4), 40:48, :].reshape(32, 128))
        expand(wide - HALO + i, right[pl.ds(i, 4), 40:48, :].reshape(32, 128))
    charges_copy.wait()
    coeff_copy.wait()

    def weigh(g, carry):
        for q in range(4):
            i = 4 * g + q
            weighted[HALO + i] = stacked(charges[i] * areas[pl.ds(i, 1), :])
        expand(HALO + 4 * g, coeff[g])
        return carry

    lax.fori_loop(0, leaves // 4, weigh, 0, unroll=4)
    codes_copy.wait()
    number = codes_s[2, 0]

    def pair(p):
        code = codes_s[0, p]
        weights = codes_s[1, p]
        column = code // 65536
        row_1 = (code // 256) % 256
        row_2 = code % 256
        points = cols_b[column]
        x_1 = rows_b[pl.ds(pl.multiple_of(row_1 * TERMS, TERMS), TERMS), :]
        x_2 = rows_b[pl.ds(pl.multiple_of(row_2 * TERMS, TERMS), TERMS), :]
        both = jnp.concatenate([x_1, x_2], axis=1)
        square = mm(points, jnp.concatenate([both] * 4, axis=0))
        inverse = lax.rsqrt(square)
        high, low = split(inverse)
        out = mm(weighted[column], jnp.concatenate([high, low], axis=0))
        out = out[:32] + out[32:]
        w_1 = (weights // 65536).astype(F32)
        w_2 = (weights % 65536).astype(F32)
        return row_1, out[:, :128] * w_1, row_2, out[:, 128:] * w_2

    def several(first, width, step, carry):
        done = [pair(first + step * width + u) for u in range(width)]
        for row_1, out_1, row_2, out_2 in done:
            field[row_1] += out_1
            field[row_2] += out_2
        return carry

    done = 0
    for width in WIDTHS:
        left_over = number - done
        steps = left_over // width if width > WIDTHS[-1] else (left_over + width - 1) // width
        lax.fori_loop(0, steps, functools.partial(several, done, width), 0)
        done = done + steps * width

    field_copy = pltpu.make_async_copy(field.at[pl.ds(0, leaves)], field_h, sems.at[6])
    field_copy.start()
    coupling_copy.wait()
    first = position * leaves
    low_at, high_at = HALO - first, leaf_total - 1 - first + HALO

    def turn_coupling(k, carry):
        for h in range(2):
            rows = jnp.concatenate([coupling_v[4 * h + q, k] for q in range(4)], axis=0)
            turned_v[pl.ds(32 * h + k, leaves, stride=64), :] = rows.T
        return carry

    lax.fori_loop(0, 32, turn_coupling, 0, unroll=8)

    def far_leaf(leaf):
        parts = [ext[jnp.clip(leaf + far_offsets[f, leaf], low_at, high_at)] for f in range(8)]
        even = lane_group(parts[0].shape) % 2 == 0
        rows = [jnp.where(even, parts[f], parts[4 + f]) for f in range(4)]
        rows = jnp.concatenate(rows, axis=0).astype(BF16)
        high, low = split(turned_v[pl.ds(pl.multiple_of(64 * leaf, 64), 64), :])
        out = mm(
            jnp.concatenate([rows, rows], axis=1),
            jnp.concatenate([high, high, low, low], axis=0),
        )
        return group_sum(by_group([out[32 * q : 32 * q + 32] for q in range(4)]))

    def far_four(g, carry):
        far[g] = by_group([far_leaf(4 * g + q) for q in range(4)])
        return carry

    lax.fori_loop(0, leaves // 4, far_four, 0, unroll=8)
    far_copy = pltpu.make_async_copy(far, far_h.at[pl.ds(0, leaves // 4)], sems.at[7])
    far_copy.start()
    field_copy.wait()
    far_copy.wait()


def final_kernel(portion_v, top_v, t_high_v, t_low_v, basis_v, near, far, out, *scratch):
    near_v, out_v, far_v, sem, far_sem, out_sems = scratch
    leaves = basis_v.shape[0]
    near_copy = pltpu.make_async_copy(near, near_v, sem)
    near_copy.start()
    far_copy = pltpu.make_async_copy(far.at[pl.ds(0, leaves // 4)], far_v, far_sem)
    far_copy.start()
    total = jnp.zeros((128, 128), F32)
    for s in range(0, 8, 2):
        blocks = [jnp.concatenate([top_v[8 * q + s + i] for q in range(4)], axis=0) for i in range(2)]
        c_high, c_low = split(jnp.concatenate(blocks, axis=1))
        p_high, p_low = split(jnp.concatenate([portion_v[:, s + i, :] for i in range(2)], axis=0))
        both = mm(jnp.concatenate([c_high, c_low], axis=0), p_high)
        total = total + both[:128] + both[128:] + mm(c_high, p_low)
    root = turned(group_sum(by_group([total[32 * q : 32 * q + 32] for q in range(4)])))
    root = jnp.where(lane_group(root.shape) == 0, root, 0.0)
    root_high, root_low = split(root)
    roots = jnp.concatenate([root_high, root_low], axis=0)
    near_copy.wait()
    far_copy.wait()

    def final(g, carry):
        at = pl.ds(pl.multiple_of(128 * g, 128), 128)
        down = mm(roots, jnp.concatenate([t_high_v[at, :], t_low_v[at, :]], axis=0), NT)
        down = down[:32, :128] + down[32:, :128] + down[:32, 128:]
        value = far_v[g] + down
        group = lane_group(value.shape)
        spread = jnp.concatenate([jnp.where(group == q, value, 0.0) for q in range(4)], axis=0)
        high, low = split(spread)
        b_high, b_low = split(basis_v[pl.ds(4 * g, 4)].reshape(128, 128))
        res = mm(jnp.concatenate([high, low], axis=1), jnp.concatenate([b_high, b_high], axis=0))
        res = res + mm(high, b_low)
        out_v[pl.ds(4 * g, 4)] = near_v[pl.ds(4 * g, 4)] + res.reshape(4, 32, 128)
        return carry

    stores = []
    part = leaves // CHUNKS
    for c in range(CHUNKS):
        lax.fori_loop(c * part // 4, (c + 1) * part // 4, final, 0, unroll=8)
        here = pl.ds(c * part, part)
        stores.append(pltpu.make_async_copy(out_v.at[here], out.at[here], out_sems.at[c]))
        stores[-1].start()
    for copy in stores:
        copy.wait()


VMEM = pl.BlockSpec(memory_space=pltpu.VMEM)
SMEM = pl.BlockSpec(memory_space=pltpu.SMEM)
ANY = pl.BlockSpec(memory_space=pltpu.HBM)
PARAMS = pltpu.CompilerParams(vmem_limit_bytes=56 * 1024 * 1024)


def struct(*shape, dtype=F32):
    return jax.ShapeDtypeStruct(shape, dtype)


def local(
    coords,
    areas,
    charges,
    near_offsets,
    near_count,
    far_offsets,
    far_coupling,
    basis,
    root_transfer,
    top_coupling,
    task_source,
    task_row,
    task_col,
):
    devices = lax.axis_size("leaf")
    position = lax.axis_index("leaf")
    leaves = coords.shape[0]
    wide = leaves + 2 * HALO
    coords = coords.transpose(1, 0, 2)
    transfer = root_transfer.transpose(1, 2, 0)
    top = top_coupling[0].transpose(1, 2, 0)
    coupling = far_coupling.transpose(1, 2, 3, 0)
    rows = leaves * 32
    coeff, t_high, t_low, roots, head, tail = pl.pallas_call(
        roots_kernel,
        out_shape=[
            struct(leaves // 4, 32, 128),
            struct(rows, 128, dtype=BF16),
            struct(rows, 128, dtype=BF16),
            struct(devices, 8, 128),
            struct(HALO, PACK, 128),
            struct(HALO, PACK, 128),
        ],
        in_specs=[VMEM, VMEM, ANY, ANY, VMEM],
        out_specs=[ANY] * 6,
        scratch_shapes=[
            pltpu.VMEM((leaves, 32, 128), F32),
            pltpu.VMEM((leaves, 32, 128), F32),
            pltpu.VMEM((leaves // 4, 32, 128), F32),
            pltpu.VMEM((leaves * 8, 128), F32),
            pltpu.VMEM((rows, 128), BF16),
            pltpu.VMEM((rows, 128), BF16),
            pltpu.VMEM((devices, 8, 128), F32),
            pltpu.VMEM((HALO, PACK, 128), F32),
            pltpu.VMEM((HALO, PACK, 128), F32),
            pltpu.SemaphoreType.DMA((2 * CHUNKS,)),
            pltpu.SemaphoreType.DMA((3 * CHUNKS + 3,)),
        ],
        compiler_params=PARAMS,
        name="coefficients",
    )(coords, areas, charges, basis, transfer)
    left = lax.ppermute(tail, "leaf", [(i, (i + 1) % devices) for i in range(devices)])
    right = lax.ppermute(head, "leaf", [((i + 1) % devices, i) for i in range(devices)])
    portion = lax.all_to_all(roots, "leaf", 0, 0, tiled=True)
    near, far = pl.pallas_call(
        functools.partial(near_kernel, leaves * devices),
        out_shape=[struct(leaves, 32, 128), struct(FAR_ROOM, 32, 128)],
        in_specs=[SMEM, SMEM, VMEM, VMEM] + [ANY] * 4 + [VMEM] * 5 + [ANY],
        out_specs=[ANY, ANY],
        scratch_shapes=[
            pltpu.VMEM((leaves // 4, 32, 128), F32),
            pltpu.VMEM((leaves + 8, 32, 128), F32),
            pltpu.VMEM((leaves, 32, 128), F32),
            pltpu.VMEM((leaves // 4, 32, 128), F32),
            pltpu.VMEM((leaves * TERMS, 128), F32),
            pltpu.VMEM((wide * TERMS, 128), F32),
            pltpu.VMEM(((leaves + 1) * TERMS, 128), BF16),
            pltpu.VMEM((wide, 128, 128), BF16),
            pltpu.VMEM((wide, 64, 256), BF16),
            pltpu.VMEM((wide, 32, 128), F32),
            pltpu.VMEM((8, 32, 32, leaves), F32),
            pltpu.VMEM((leaves * 64, 128), F32),
            pltpu.VMEM((2, HALO, PACK, 128), F32),
            pltpu.VMEM((8, 768), jnp.int32),
            pltpu.SMEM((8, 768), jnp.int32),
            pltpu.SemaphoreType.DMA((8,)),
        ],
        compiler_params=PARAMS,
        cost_estimate=pl.CostEstimate(flops=3 * 10**10, bytes_accessed=3 * 10**7, transcendentals=10**7),
        name="near",
    )(
        position.reshape(1),
        far_offsets.T,
        coords,
        areas,
        charges,
        coeff,
        left,
        right,
        near_offsets.T,
        near_count.reshape(1, leaves),
        task_source.reshape(devices, -1),
        task_row.reshape(devices, -1),
        task_col.reshape(devices, -1),
        coupling,
    )
    return pl.pallas_call(
        final_kernel,
        out_shape=struct(leaves, 32, 128),
        in_specs=[VMEM] * 5 + [ANY, ANY],
        out_specs=ANY,
        scratch_shapes=[
            pltpu.VMEM((leaves, 32, 128), F32),
            pltpu.VMEM((leaves, 32, 128), F32),
            pltpu.VMEM((leaves // 4, 32, 128), F32),
            pltpu.SemaphoreType.DMA,
            pltpu.SemaphoreType.DMA,
            pltpu.SemaphoreType.DMA((CHUNKS,)),
        ],
        input_output_aliases={5: 0},
        compiler_params=pltpu.CompilerParams(vmem_limit_bytes=16 * 1024 * 1024),
        name="final",
    )(portion, top, t_high, t_low, basis, near, far)


def solution(mesh):
    placed = (
        P("leaf", None, None),
        P("leaf", None),
        P("leaf", None, None),
        P("leaf", None),
        P("leaf"),
        P("leaf", None),
        P("leaf", None, None, None),
        P("leaf", None, None),
        P("leaf", None, None),
        P("leaf", None, None, None),
        P(),
        P(),
        P(),
    )
    return jax.shard_map(
        local, mesh=mesh, in_specs=placed, out_specs=P("leaf", None, None), check_vma=False
    )
```

```python
import functools

import jax
import jax.numpy as jnp
from jax import lax
from jax.experimental import pallas as pl
from jax.experimental.pallas import tpu as pltpu
from jax.sharding import PartitionSpec as P

HALO = 8
SOFTENING = 0.001
F32 = jnp.float32
BF16 = jnp.bfloat16
TERMS = 32
PACK = 48
NT = (((1,), (1,)), ((), ()))
NN = (((1,), (0,)), ((), ()))
TN = (((0,), (0,)), ((), ()))


def mm(a, b, dims=NN):
    return lax.dot_general(a, b, dims, preferred_element_type=F32)


def split(x):
    high = x.astype(BF16)
    return high, (x - high.astype(F32)).astype(BF16)


def stacked(x):
    high, low = split(x)
    top = jnp.concatenate([high, high], axis=1)
    bottom = jnp.concatenate([low, jnp.zeros_like(low)], axis=1)
    return jnp.concatenate([top, bottom], axis=0)


def lane_group(shape):
    return lax.broadcasted_iota(jnp.int32, shape, 1) // 32


def by_group(parts):
    group = lane_group(parts[0].shape)
    low = jnp.where(group == 0, parts[0], parts[1])
    high = jnp.where(group == 2, parts[2], parts[3])
    return jnp.where(group < 2, low, high)


def turned(x):
    return jnp.concatenate([x] * 4, axis=0).T[:32]


def group_sum(x):
    x = x + pltpu.roll(x, 64, 1)
    return x + pltpu.roll(x, 32, 1)


CHUNKS = 2
WIDTHS = (64, 16, 4)
FAR_ROOM = 3200


def roots_kernel(
    coords, areas, charges, basis, transfer, coeff, t_high, t_low, roots, head, tail, *scratch
):
    charge_v, basis_v, coeff_v, turned_v, t_high_v, t_low_v, roots_v, head_v, tail_v, in_sems, out_sems = scratch
    leaves = charges.shape[0]
    part = leaves // CHUNKS
    loads = []
    for c in range(CHUNKS):
        here = pl.ds(c * part, part)
        loads.append(
            (
                pltpu.make_async_copy(charges.at[here], charge_v.at[here], in_sems.at[2 * c]),
                pltpu.make_async_copy(basis.at[here], basis_v.at[here], in_sems.at[2 * c + 1]),
            )
        )
    for pair in loads:
        for copy in pair:
            copy.start()
    for h in range(8):
        rows = jnp.concatenate([transfer[8 * q + h] for q in range(4)], axis=0)
        turned_v[pl.ds(h, leaves, stride=8), :] = rows.T
    total = jnp.zeros((64, 128), F32)
    stores = []

    def four(g, total):
        leaf = 4 * g
        values = jnp.concatenate([stacked(charge_v[leaf + q]) for q in range(4)], axis=0)
        bases = jnp.concatenate(split(basis_v[pl.ds(leaf, 4)].reshape(128, 128)), axis=1)
        out = mm(values, bases, NT)
        value = by_group([out[64 * q : 64 * q + 32] + out[64 * q + 32 : 64 * q + 64] for q in range(4)])
        coeff_v[g] = value
        for q in range(4):
            tile = turned_v[pl.ds(pl.multiple_of(8 * (leaf + q), 8), 8), :]
            tile = jnp.concatenate([tile] + [pltpu.roll(tile, 128 - 32 * k, 1) for k in (1, 2, 3)], axis=0)
            high, low = split(tile)
            at = pl.ds(pl.multiple_of(32 * (leaf + q), 32), 32)
            t_high_v[at, :] = high
            t_low_v[at, :] = low
        high, low = split(value)
        at = pl.ds(pl.multiple_of(128 * g, 128), 128)
        total = total + mm(jnp.concatenate([high, low], axis=0), t_high_v[at, :])
        rest = mm(high, t_low_v[at, :])
        return total + jnp.concatenate([rest, jnp.zeros_like(rest)], axis=0)

    for c in range(CHUNKS):
        for copy in loads[c]:
            copy.wait()
        total = lax.fori_loop(c * part // 4, (c + 1) * part // 4, four, total, unroll=8)
        here = pl.ds(c * part // 4, part // 4)
        rows = pl.ds(c * part * 32, part * 32)
        for source, target in ((coeff_v.at[here], coeff.at[here]), (t_high_v.at[rows], t_high.at[rows]), (t_low_v.at[rows], t_low.at[rows])):
            copy = pltpu.make_async_copy(source, target, out_sems.at[len(stores)])
            copy.start()
            stores.append(copy)
    total = turned(total[:32] + total[32:])
    packed = by_group([total[8 * g : 8 * g + 8] for g in range(4)])
    roots_v[...] = jnp.broadcast_to(packed[None], roots_v.shape)
    copy = pltpu.make_async_copy(roots_v, roots, out_sems.at[len(stores)])
    copy.start()
    stores.append(copy)
    for out, out_v, first in ((head, head_v, 0), (tail, tail_v, leaves - HALO)):
        for i in range(HALO):
            out_v[i, 0:32, :] = charge_v[first + i] * areas[pl.ds(first + i, 1), :]
            out_v[i, 40:48, :] = coeff_v[first // 4 + i // 4, pl.ds(8 * (i % 4), 8), :]
        out_v[:, 32:40, :] = jnp.zeros((HALO, 8, 128), F32)
        for k in range(3):
            out_v[:, 32 + k, :] = coords[k, pl.ds(first, HALO), :]
        copy = pltpu.make_async_copy(out_v, out, out_sems.at[len(stores)])
        copy.start()
        stores.append(copy)
    for copy in stores:
        copy.wait()


def terms(comps, rows):
    coarse = [jnp.floor(x * 128.0 + 0.5) * (1.0 / 128.0) for x in comps]
    fine = [x - q for x, q in zip(comps, coarse)]
    fine_high = [r.astype(BF16).astype(F32) for r in fine]
    fine_low = [r - h for r, h in zip(fine, fine_high)]
    square = sum(q * q for q in coarse)
    square_high = square.astype(BF16).astype(F32)
    square_low = square - square_high
    rest = sum(2.0 * q * r + r * r for q, r in zip(coarse, fine))
    if rows:
        rest = rest + SOFTENING
    rest_1 = rest.astype(BF16).astype(F32)
    rest_2 = (rest - rest_1).astype(BF16).astype(F32)
    rest_3 = rest - rest_1 - rest_2
    one = jnp.ones_like(square)
    zero = jnp.zeros_like(square)
    if rows:
        coarse = [-2.0 * x for x in coarse]
        fine_high = [-2.0 * x for x in fine_high]
        fine_low = [-2.0 * x for x in fine_low]
        own = [square_high, square_low, one, one]
        own2 = [rest_1, rest_2, rest_3, one, one, one]
        return own + coarse + [zero] + own2 + fine_high + fine_low + coarse + coarse + fine_high + fine_low
    own = [one, one, square_high, square_low]
    own2 = [one, one, one, rest_1, rest_2, rest_3]
    return own + coarse + [zero] + own2 + coarse + coarse + fine_high + fine_low + fine_high + fine_high


def build_lists(position, leaves, leaf_total, near_offsets, near_count, task_source, task_row, task_col, codes):
    first = position * leaves
    low, high = HALO - first, leaf_total - 1 - first + HALO
    slots = near_offsets.shape[0]
    shape = (128, 128)
    column = lax.broadcasted_iota(jnp.int32, shape, 0)
    row = lax.broadcasted_iota(jnp.int32, shape, 1)
    spare = 128 - leaves
    offsets = jnp.concatenate([near_offsets[...], jnp.zeros((slots, spare), jnp.int32)], axis=1)
    count = jnp.concatenate([near_count[...], jnp.zeros((1, spare), jnp.int32)], axis=1)
    near = jnp.zeros(shape, F32)
    for s in range(slots):
        at = jnp.clip(offsets[s : s + 1] + row[0:1], low, high)
        at = jnp.where(count > s, at, -1)
        near = near + jnp.where(column == at, 1.0, 0.0)
    mine = task_source[...] == position
    at = jnp.clip(task_col[...], low, high)
    value = jnp.where(mine, task_row[...] * 128 + at + 1, 0).astype(F32)
    largest = jnp.max(value, axis=1, keepdims=True)
    other = jnp.sum(value, axis=1, keepdims=True) - largest
    listed = jnp.zeros(shape, F32)
    lanes = lax.broadcasted_iota(jnp.int32, (value.shape[0], 128), 1)
    for value in (largest, other):
        task = value.astype(jnp.int32) - 1
        t_row = jnp.where(task < 0, -1, task // 128)
        t_col = jnp.where(task < 0, -1, task % 128)
        pick_row = jnp.where(lanes == t_row, 1.0, 0.0).astype(BF16)
        pick_col = jnp.where(lanes == t_col, 1.0, 0.0).astype(BF16)
        listed = listed + mm(pick_col, pick_row, TN)
    used = jnp.where(near + listed > 0.0, 1.0, 0.0)
    before = jnp.where(column < row, 1.0, 0.0).astype(BF16)
    rank = mm(used.astype(BF16), before)
    number = jnp.sum(used, axis=1, keepdims=True)
    pairs = jnp.floor((number + 1.0) * 0.5)
    after = jnp.where(row <= column, 1.0, 0.0).astype(BF16)
    pairs_wide = jnp.broadcast_to(pairs, shape)
    ends = mm(after, pairs_wide.astype(BF16))
    size = codes.shape[1]
    copies = size // 128
    ends_wide = jnp.concatenate([ends] * copies, axis=1)
    starts_wide = jnp.concatenate([ends - pairs_wide] * copies, axis=1)
    place = lax.broadcasted_iota(jnp.int32, (128, size), 1).astype(F32)
    here = jnp.where((place >= starts_wide) & (place < ends_wide), 1.0, 0.0)
    column_at = jnp.sum(jnp.where(place >= ends_wide, 1.0, 0.0), axis=0, keepdims=True)
    within = jnp.sum(here * (place - starts_wide), axis=0, keepdims=True)
    here = here.astype(BF16)
    order = (used * (rank + 1.0)).T.astype(BF16)[:leaves]
    near_t = near.T.astype(BF16)[:leaves]
    listed_t = listed.T.astype(BF16)[:leaves]
    order_at = mm(order, here)
    weight_at = mm(near_t, here) + mm(listed_t, here)
    row_at = lax.broadcasted_iota(jnp.int32, (leaves, size), 0).astype(F32)
    found = []
    for k in (1.0, 2.0):
        hit = order_at == (2.0 * within + k)
        found.append(leaves + jnp.sum(jnp.where(hit, row_at - leaves, 0.0), axis=0, keepdims=True))
        found.append(jnp.sum(jnp.where(hit, weight_at, 0.0), axis=0, keepdims=True))
    row_1, weight_1, row_2, weight_2 = [x.astype(jnp.int32) for x in found]
    total = jnp.concatenate([ends[127:128]] * copies, axis=1).astype(jnp.int32)
    column_at = jnp.minimum(column_at.astype(jnp.int32), leaves + 2 * HALO - 1)
    codes[0:1, :] = column_at * 65536 + row_1 * 256 + row_2
    codes[1:2, :] = weight_1 * 65536 + weight_2
    codes[2:3, :] = total
    codes[3:8, :] = jnp.zeros((5, size), jnp.int32)


def near_kernel(
    leaf_total,
    place,
    far_offsets,
    coords,
    areas,
    charges_h,
    coeff_h,
    left_h,
    right_h,
    near_offsets,
    near_count,
    task_source,
    task_row,
    task_col,
    coupling,
    field_h,
    far_h,
    far,
    field,
    charges,
    coeff,
    rows_f,
    cols_f,
    rows_b,
    cols_b,
    weighted,
    ext,
    coupling_v,
    turned_v,
    halo,
    codes,
    codes_s,
    sems,
):
    leaves = charges.shape[0]
    wide = leaves + 2 * HALO
    position = place[0]
    charges_copy = pltpu.make_async_copy(charges_h, charges, sems.at[4])
    coeff_copy = pltpu.make_async_copy(coeff_h, coeff, sems.at[5])
    charges_copy.start()
    coeff_copy.start()
    left, right = halo.at[0], halo.at[1]
    left_copy = pltpu.make_async_copy(left_h, left, sems.at[2])
    right_copy = pltpu.make_async_copy(right_h, right, sems.at[3])
    left_copy.start()
    right_copy.start()
    coupling_copy = pltpu.make_async_copy(coupling, coupling_v, sems.at[0])
    coupling_copy.start()
    build_lists(
        position, leaves, leaf_total, near_offsets, near_count, task_source, task_row, task_col, codes
    )
    codes_copy = pltpu.make_async_copy(codes, codes_s, sems.at[1])
    codes_copy.start()
    field[...] = jnp.zeros_like(field)

    mine = [coords[c] for c in range(3)]
    for k, value in enumerate(terms(mine, True)):
        rows_f[pl.ds(k, leaves, stride=TERMS), :] = value
    rows_b[pl.ds(0, leaves * TERMS), :] = rows_f[...].astype(BF16)
    rows_b[pl.ds(leaves * TERMS, TERMS), :] = rows_f[0:TERMS, :].astype(BF16)
    left_copy.wait()
    right_copy.wait()
    everyone = [
        jnp.concatenate([left[:, 32 + c, :], mine[c], right[:, 32 + c, :]], axis=0) for c in range(3)
    ]
    for k, value in enumerate(terms(everyone, False)):
        cols_f[pl.ds(k, wide, stride=TERMS), :] = value
    eye = jnp.where(
        lax.broadcasted_iota(jnp.int32, (128, 128), 0) == lax.broadcasted_iota(jnp.int32, (128, 128), 1),
        1.0,
        0.0,
    ).astype(BF16)

    def turn(g, carry):
        block = cols_f[pl.ds(pl.multiple_of(g * 128, 128), 128), :].astype(BF16)
        out = mm(eye, block, NT)
        for q in range(4):
            cols_b[4 * g + q] = jnp.where(lane_group(out.shape) == q, out, 0.0).astype(BF16)
        return carry

    lax.fori_loop(0, wide // 4, turn, 0, unroll=20)

    source = lax.broadcasted_iota(jnp.int32, (256, 512), 0)
    target = lax.broadcasted_iota(jnp.int32, (256, 512), 1)
    same = (source % 32 == target % 32) & ((source % 128) // 32 == target // 128)
    same = same & (source // 128 == (target % 128) // 64)
    spread = jnp.where(same, 1.0, 0.0).astype(BF16)

    def expand(first, packed):
        out = mm(jnp.concatenate(split(packed), axis=1), spread)
        for q in range(4):
            ext[first + q] = out[:, 128 * q : 128 * q + 128]

    for i in range(HALO):
        weighted[i] = stacked(left[i, 0:32, :])
        weighted[wide - HALO + i] = stacked(right[i, 0:32, :])
    for i in range(0, HALO, 4):
        expand(i, left[pl.ds(i, 4), 40:48, :].reshape(32, 128))
        expand(wide - HALO + i, right[pl.ds(i, 4), 40:48, :].reshape(32, 128))
    charges_copy.wait()
    coeff_copy.wait()

    def weigh(g, carry):
        for q in range(4):
            i = 4 * g + q
            weighted[HALO + i] = stacked(charges[i] * areas[pl.ds(i, 1), :])
        expand(HALO + 4 * g, coeff[g])
        return carry

    lax.fori_loop(0, leaves // 4, weigh, 0, unroll=16)
    codes_copy.wait()
    number = codes_s[2, 0]

    def pair(p):
        code = codes_s[0, p]
        weights = codes_s[1, p]
        column = code // 65536
        row_1 = (code // 256) % 256
        row_2 = code % 256
        points = cols_b[column]
        x_1 = rows_b[pl.ds(pl.multiple_of(row_1 * TERMS, TERMS), TERMS), :]
        x_2 = rows_b[pl.ds(pl.multiple_of(row_2 * TERMS, TERMS), TERMS), :]
        both = jnp.concatenate([x_1, x_2], axis=1)
        square = mm(points, jnp.concatenate([both] * 4, axis=0))
        inverse = lax.rsqrt(square)
        high, low = split(inverse)
        out = mm(weighted[column], jnp.concatenate([high, low], axis=0))
        out = out[:32] + out[32:]
        w_1 = (weights // 65536).astype(F32)
        w_2 = (weights % 65536).astype(F32)
        return row_1, out[:, :128] * w_1, row_2, out[:, 128:] * w_2

    def several(first, width, step, carry):
        done = [pair(first + step * width + u) for u in range(width)]
        for row_1, out_1, row_2, out_2 in done:
            field[row_1] += out_1
            field[row_2] += out_2
        return carry

    done = 0
    for width in WIDTHS:
        left_over = number - done
        steps = left_over // width if width > WIDTHS[-1] else (left_over + width - 1) // width
        lax.fori_loop(0, steps, functools.partial(several, done, width), 0)
        done = done + steps * width

    field_copy = pltpu.make_async_copy(field.at[pl.ds(0, leaves)], field_h, sems.at[6])
    field_copy.start()
    coupling_copy.wait()
    first = position * leaves
    low_at, high_at = HALO - first, leaf_total - 1 - first + HALO

    def turn_coupling(k, carry):
        for h in range(2):
            rows = jnp.concatenate([coupling_v[4 * h + q, k] for q in range(4)], axis=0)
            turned_v[pl.ds(32 * h + k, leaves, stride=64), :] = rows.T
        return carry

    lax.fori_loop(0, 32, turn_coupling, 0, unroll=16)

    def far_leaf(leaf):
        parts = [ext[jnp.clip(leaf + far_offsets[f, leaf], low_at, high_at)] for f in range(8)]
        even = lane_group(parts[0].shape) % 2 == 0
        rows = [jnp.where(even, parts[f], parts[4 + f]) for f in range(4)]
        rows = jnp.concatenate(rows, axis=0).astype(BF16)
        high, low = split(turned_v[pl.ds(pl.multiple_of(64 * leaf, 64), 64), :])
        out = mm(
            jnp.concatenate([rows, rows], axis=1),
            jnp.concatenate([high, high, low, low], axis=0),
        )
        return group_sum(by_group([out[32 * q : 32 * q + 32] for q in range(4)]))

    def far_four(g, carry):
        far[g] = by_group([far_leaf(4 * g + q) for q in range(4)])
        return carry

    lax.fori_loop(0, leaves // 4, far_four, 0, unroll=16)
    far_copy = pltpu.make_async_copy(far, far_h.at[pl.ds(0, leaves // 4)], sems.at[7])
    far_copy.start()
    field_copy.wait()
    far_copy.wait()


def final_kernel(portion_v, top_v, t_high_v, t_low_v, basis_v, near, far, out, *scratch):
    near_v, out_v, far_v, sem, far_sem, out_sems = scratch
    leaves = basis_v.shape[0]
    near_copy = pltpu.make_async_copy(near, near_v, sem)
    near_copy.start()
    far_copy = pltpu.make_async_copy(far.at[pl.ds(0, leaves // 4)], far_v, far_sem)
    far_copy.start()
    total = jnp.zeros((128, 128), F32)
    for s in range(0, 8, 2):
        blocks = [jnp.concatenate([top_v[8 * q + s + i] for q in range(4)], axis=0) for i in range(2)]
        c_high, c_low = split(jnp.concatenate(blocks, axis=1))
        p_high, p_low = split(jnp.concatenate([portion_v[:, s + i, :] for i in range(2)], axis=0))
        both = mm(jnp.concatenate([c_high, c_low], axis=0), p_high)
        total = total + both[:128] + both[128:] + mm(c_high, p_low)
    root = turned(group_sum(by_group([total[32 * q : 32 * q + 32] for q in range(4)])))
    root = jnp.where(lane_group(root.shape) == 0, root, 0.0)
    root_high, root_low = split(root)
    roots = jnp.concatenate([root_high, root_low], axis=0)
    near_copy.wait()
    far_copy.wait()

    def final(g, carry):
        at = pl.ds(pl.multiple_of(128 * g, 128), 128)
        down = mm(roots, jnp.concatenate([t_high_v[at, :], t_low_v[at, :]], axis=0), NT)
        down = down[:32, :128] + down[32:, :128] + down[:32, 128:]
        value = far_v[g] + down
        group = lane_group(value.shape)
        spread = jnp.concatenate([jnp.where(group == q, value, 0.0) for q in range(4)], axis=0)
        high, low = split(spread)
        b_high, b_low = split(basis_v[pl.ds(4 * g, 4)].reshape(128, 128))
        res = mm(jnp.concatenate([high, low], axis=1), jnp.concatenate([b_high, b_high], axis=0))
        res = res + mm(high, b_low)
        out_v[pl.ds(4 * g, 4)] = near_v[pl.ds(4 * g, 4)] + res.reshape(4, 32, 128)
        return carry

    stores = []
    part = leaves // CHUNKS
    for c in range(CHUNKS):
        lax.fori_loop(c * part // 4, (c + 1) * part // 4, final, 0, unroll=8)
        here = pl.ds(c * part, part)
        stores.append(pltpu.make_async_copy(out_v.at[here], out.at[here], out_sems.at[c]))
        stores[-1].start()
    for copy in stores:
        copy.wait()


VMEM = pl.BlockSpec(memory_space=pltpu.VMEM)
SMEM = pl.BlockSpec(memory_space=pltpu.SMEM)
ANY = pl.BlockSpec(memory_space=pltpu.HBM)
PARAMS = pltpu.CompilerParams(vmem_limit_bytes=56 * 1024 * 1024)


def struct(*shape, dtype=F32):
    return jax.ShapeDtypeStruct(shape, dtype)


def local(
    coords,
    areas,
    charges,
    near_offsets,
    near_count,
    far_offsets,
    far_coupling,
    basis,
    root_transfer,
    top_coupling,
    task_source,
    task_row,
    task_col,
):
    devices = lax.axis_size("leaf")
    position = lax.axis_index("leaf")
    leaves = coords.shape[0]
    wide = leaves + 2 * HALO
    coords = coords.transpose(1, 0, 2)
    transfer = root_transfer.transpose(1, 2, 0)
    top = top_coupling[0].transpose(1, 2, 0)
    coupling = far_coupling.transpose(1, 2, 3, 0)
    rows = leaves * 32
    coeff, t_high, t_low, roots, head, tail = pl.pallas_call(
        roots_kernel,
        out_shape=[
            struct(leaves // 4, 32, 128),
            struct(rows, 128, dtype=BF16),
            struct(rows, 128, dtype=BF16),
            struct(devices, 8, 128),
            struct(HALO, PACK, 128),
            struct(HALO, PACK, 128),
        ],
        in_specs=[VMEM, VMEM, ANY, ANY, VMEM],
        out_specs=[ANY] * 6,
        scratch_shapes=[
            pltpu.VMEM((leaves, 32, 128), F32),
            pltpu.VMEM((leaves, 32, 128), F32),
            pltpu.VMEM((leaves // 4, 32, 128), F32),
            pltpu.VMEM((leaves * 8, 128), F32),
            pltpu.VMEM((rows, 128), BF16),
            pltpu.VMEM((rows, 128), BF16),
            pltpu.VMEM((devices, 8, 128), F32),
            pltpu.VMEM((HALO, PACK, 128), F32),
            pltpu.VMEM((HALO, PACK, 128), F32),
            pltpu.SemaphoreType.DMA((2 * CHUNKS,)),
            pltpu.SemaphoreType.DMA((3 * CHUNKS + 3,)),
        ],
        compiler_params=PARAMS,
        name="coefficients",
    )(coords, areas, charges, basis, transfer)
    left = lax.ppermute(tail, "leaf", [(i, (i + 1) % devices) for i in range(devices)])
    right = lax.ppermute(head, "leaf", [((i + 1) % devices, i) for i in range(devices)])
    portion = lax.all_to_all(roots, "leaf", 0, 0, tiled=True)
    near, far = pl.pallas_call(
        functools.partial(near_kernel, leaves * devices),
        out_shape=[struct(leaves, 32, 128), struct(FAR_ROOM, 32, 128)],
        in_specs=[SMEM, SMEM, VMEM, VMEM] + [ANY] * 4 + [VMEM] * 5 + [ANY],
        out_specs=[ANY, ANY],
        scratch_shapes=[
            pltpu.VMEM((leaves // 4, 32, 128), F32),
            pltpu.VMEM((leaves + 8, 32, 128), F32),
            pltpu.VMEM((leaves, 32, 128), F32),
            pltpu.VMEM((leaves // 4, 32, 128), F32),
            pltpu.VMEM((leaves * TERMS, 128), F32),
            pltpu.VMEM((wide * TERMS, 128), F32),
            pltpu.VMEM(((leaves + 1) * TERMS, 128), BF16),
            pltpu.VMEM((wide, 128, 128), BF16),
            pltpu.VMEM((wide, 64, 256), BF16),
            pltpu.VMEM((wide, 32, 128), F32),
            pltpu.VMEM((8, 32, 32, leaves), F32),
            pltpu.VMEM((leaves * 64, 128), F32),
            pltpu.VMEM((2, HALO, PACK, 128), F32),
            pltpu.VMEM((8, 768), jnp.int32),
            pltpu.SMEM((8, 768), jnp.int32),
            pltpu.SemaphoreType.DMA((8,)),
        ],
        compiler_params=PARAMS,
        cost_estimate=pl.CostEstimate(flops=3 * 10**10, bytes_accessed=3 * 10**7, transcendentals=10**7),
        name="near",
    )(
        position.reshape(1),
        far_offsets.T,
        coords,
        areas,
        charges,
        coeff,
        left,
        right,
        near_offsets.T,
        near_count.reshape(1, leaves),
        task_source.reshape(devices, -1),
        task_row.reshape(devices, -1),
        task_col.reshape(devices, -1),
        coupling,
    )
    return pl.pallas_call(
        final_kernel,
        out_shape=struct(leaves, 32, 128),
        in_specs=[VMEM] * 5 + [ANY, ANY],
        out_specs=ANY,
        scratch_shapes=[
            pltpu.VMEM((leaves, 32, 128), F32),
            pltpu.VMEM((leaves, 32, 128), F32),
            pltpu.VMEM((leaves // 4, 32, 128), F32),
            pltpu.SemaphoreType.DMA,
            pltpu.SemaphoreType.DMA,
            pltpu.SemaphoreType.DMA((CHUNKS,)),
        ],
        input_output_aliases={5: 0},
        compiler_params=pltpu.CompilerParams(vmem_limit_bytes=16 * 1024 * 1024),
        name="final",
    )(portion, top, t_high, t_low, basis, near, far)


def solution(mesh):
    placed = (
        P("leaf", None, None),
        P("leaf", None),
        P("leaf", None, None),
        P("leaf", None),
        P("leaf"),
        P("leaf", None),
        P("leaf", None, None, None),
        P("leaf", None, None),
        P("leaf", None, None),
        P("leaf", None, None, None),
        P(),
        P(),
        P(),
    )
    return jax.shard_map(
        local, mesh=mesh, in_specs=placed, out_specs=P("leaf", None, None), check_vma=False
    )
```
